32 devices in a mesh: dom: 8 (over z, x), local: 4 (over y, core).
Axes of the slice: x: 2, y: 2, z: 4, core: 2. Of those that a mesh axis runs over, the one named last changes fastest.
Arguments:
- features: bfloat16 [65536, 128], P(('dom', 'local')), may hold values from -6 to 6
- serve_rows: int32 [256, 4], P(('dom', 'local')), may hold values from 0 to 2047
- pick_rows: int32 [128, 128], P(('dom', 'local')), may hold values from 0 to 31
- neighbours: int32 [32768, 15], P(('dom', 'local')), may hold values from 0 to 511
- batch_nodes: int32 [32768], P(('dom', 'local')), may hold values from 0 to 2047
- w_self: bfloat16 [128, 256], replicated, may hold values from -0.5 to 0.5
- w_neigh: bfloat16 [128, 256], replicated, may hold values from -1 to 1
- cotangent: bfloat16 [32768, 256], P(('dom', 'local')), may hold values from -6 to 6
Outputs:
- hidden: bfloat16 [32768, 256], P(('dom', 'local'))
- grad_self: float32 [128, 256], replicated
- grad_neigh: float32 [128, 256], replicated
The draws below stay inside these ranges and needn't reach their ends.
All inputs are finite; a program needn't handle non-finite values.
Results may differ from the reference program's by a relative error of at most 0.0051.
Values may be sent and summed in bfloat16 or wider, within the bound.
No kernel may reach another device: no remote copies, remote signals or barrier semaphores. Data moves between devices by JAX's collectives and lax.ppermute only.
A program may use at most 64 MiB of HBM per device.

```python
import math
import jax
import jax.numpy as jnp
import numpy as np
from jax import lax

F = 128
H = 256
FANOUT = 15
CAP = 4
NODES_DEV = 2048
BATCH = 1024
CAP2 = 128
POOL = 512
NB = 32
N_DOM = 8
N_LOCAL = 4
DEVICES = 32


def set_ends(values, stream_key, smallest, largest):
    spot = [jax.random.randint(jax.random.fold_in(stream_key, axis), (), 0, length) for axis, length in enumerate(values.shape)]
    main_axis = values.shape.index(max(values.shape))
    neighbour = spot[:main_axis] + [(spot[main_axis] + 1) % values.shape[main_axis]] + spot[main_axis + 1:]
    return values.at[tuple(spot)].set(smallest).at[tuple(neighbour)].set(largest)


def level_of(own_key, dims, cuts, low, high):
    gain = 1.0
    for axis_at, shards_of in cuts:
        heights = jax.random.uniform(jax.random.fold_in(jax.random.fold_in(own_key, 6), axis_at), (shards_of,), jnp.float32, low / len(cuts), high / len(cuts))
        gain = gain * jnp.repeat(jnp.exp(heights), dims[axis_at] // shards_of).reshape((-1,) + (1,) * (len(dims) - 1 - axis_at))
    return gain


def rank_table(count, lean):
    loads = [(1 << 20) // math.isqrt(rank ** lean) + 1 for rank in range(1, count + 1)]
    spread = 1 + sum(loads) // (1 << 30)
    return np.cumsum(np.array([max(1, weight // spread) for weight in loads]))


def ranked_ids(stream_key, extent, number_of, skew):
    listing = rank_table(number_of, skew)
    lot = jax.random.randint(jax.random.fold_in(stream_key, 1), extent, 0, int(listing[number_of - 1]))
    rank = jnp.searchsorted(jnp.asarray(listing, jnp.int32), lot, side="right")
    return jax.random.permutation(jax.random.fold_in(stream_key, 2), number_of)[rank].astype(jnp.int32)


def scatter_about(stream_key, extent, scale, bound, pieces=(), kind=jnp.bfloat16):
    array = scale * jax.random.normal(stream_key, extent, jnp.float32)
    if pieces:
        array = array * level_of(stream_key, extent, pieces, -0.22, 0.18)
    return jnp.clip(array, -bound, bound).astype(kind)


def setup_inputs(seed: int = 0) -> dict:
    key_of = jax.random.split(jax.random.key(seed), 9)
    return {
        "features": scatter_about(key_of[0], (DEVICES * NODES_DEV, F), 1.0, 6.0, ((0, 32),)),
        "serve_rows": set_ends(ranked_ids(key_of[1], (DEVICES * N_DOM, CAP), NODES_DEV, 2), jax.random.fold_in(key_of[1], 3), 0, NODES_DEV - 1).astype(jnp.int32),
        "pick_rows": set_ends(jax.random.randint(key_of[2], (DEVICES * N_LOCAL, CAP2), 0, NB), jax.random.fold_in(key_of[2], 1), 0, NB - 1).astype(jnp.int32),
        "neighbours": set_ends(ranked_ids(key_of[3], (DEVICES * BATCH, FANOUT), POOL, 1), jax.random.fold_in(key_of[3], 3), 0, POOL - 1).astype(jnp.int32),
        "batch_nodes": set_ends(jax.random.randint(key_of[4], (DEVICES * BATCH,), 0, NODES_DEV), jax.random.fold_in(key_of[4], 1), 0, NODES_DEV - 1).astype(jnp.int32),
        "w_self": scatter_about(key_of[5], (F, H), F ** -0.5, 0.5),
        "w_neigh": scatter_about(key_of[6], (F, H), (F // 4) ** -0.5, 1.0),
        "cotangent": scatter_about(key_of[7], (DEVICES * BATCH, H), 1.0, 6.0, ((0, 32),)),
    }


def reference(features, serve_rows, pick_rows, neighbours, batch_nodes, w_self, w_neigh, cotangent):
    trainers = N_DOM * N_LOCAL
    served = serve_rows.reshape(N_DOM, N_LOCAL, N_DOM, CAP).astype(jnp.int32)
    owner_base = (jnp.arange(N_DOM, dtype=jnp.int32)[:, None] * N_LOCAL + jnp.arange(N_LOCAL, dtype=jnp.int32)[None, :]) * NODES_DEV
    global_rows = served + owner_base[:, :, None, None]
    collected_ids = jnp.transpose(global_rows, (2, 1, 0, 3)).reshape(trainers * NB)
    picks = pick_rows.reshape(N_DOM, N_LOCAL, N_LOCAL, CAP2).astype(jnp.int32)
    source_base = (jnp.arange(N_DOM, dtype=jnp.int32)[:, None, None, None] * N_LOCAL + jnp.arange(N_LOCAL, dtype=jnp.int32)[None, None, :, None]) * NB
    pool_ids = collected_ids[(picks + source_base).reshape(-1)].reshape(trainers, POOL)
    scale = 1.0 / math.sqrt(trainers * BATCH)
    nbr_all = neighbours.reshape(trainers, BATCH, FANOUT).astype(jnp.int32)
    batch_all = batch_nodes.reshape(trainers, BATCH).astype(jnp.int32)
    cot_all = cotangent.reshape(trainers, BATCH, H)
    indices = jnp.arange(trainers, dtype=jnp.int32)

    def one_trainer(carry, inputs):
        ids, nbr, batch_rows, cot, index = inputs
        rows = features[ids[nbr]]
        neighbour_mean = (lax.optimization_barrier(jnp.sum(rows.astype(jnp.float32), axis=1)) / FANOUT).astype(jnp.bfloat16)
        self_rows = features[index * NODES_DEV + batch_rows]
        pre = jnp.dot(self_rows, w_self, preferred_element_type=jnp.float32) + jnp.dot(neighbour_mean, w_neigh, preferred_element_type=jnp.float32)
        sigma = jax.nn.sigmoid(pre)
        hidden = (pre * sigma).astype(jnp.bfloat16)
        slope = (cot.astype(jnp.float32) * sigma * (1.0 + pre * (1.0 - sigma))).astype(jnp.bfloat16)
        term_self = jnp.dot(self_rows.T, slope, preferred_element_type=jnp.float32) * scale
        term_neigh = jnp.dot(neighbour_mean.T, slope, preferred_element_type=jnp.float32) * scale
        return ((carry[0] + term_self, carry[1] + term_neigh), hidden)
    start = (jnp.zeros((F, H), jnp.float32), jnp.zeros((F, H), jnp.float32))
    totals, hidden_all = lax.scan(one_trainer, start, (pool_ids, nbr_all, batch_all, cot_all, indices))
    return (hidden_all.reshape(trainers * BATCH, H), totals[0], totals[1])
```

```python
import functools
import math

import jax
import jax.numpy as jnp
from jax import lax
from jax.experimental import pallas as pl
from jax.experimental.pallas import tpu as pltpu
from jax.sharding import PartitionSpec as P

AXES = ("dom", "local")
LANES = 128
VMEM = pl.BlockSpec(memory_space=pltpu.VMEM)


def call(kernel, out_shape, operands, flops, bytes_accessed, scratch=()):
    return pl.pallas_call(
        kernel,
        out_shape=out_shape,
        in_specs=[VMEM] * len(operands),
        out_specs=jax.tree.map(lambda _: VMEM, out_shape),
        scratch_shapes=list(scratch),
        compiler_params=pltpu.CompilerParams(vmem_limit_bytes=40 * 2**20),
        cost_estimate=pl.CostEstimate(
            flops=flops, bytes_accessed=bytes_accessed, transcendentals=0
        ),
    )(*operands)


def serve_kernel(n_local, serve_ref, features_ref, out_ref):
    cap, n_dom = serve_ref.shape
    n_nodes = features_ref.shape[0]
    serve = serve_ref[...].astype(jnp.float32)
    block = 128
    for base in range(0, out_ref.shape[0], block):
        row = base + lax.broadcasted_iota(jnp.int32, (block, n_dom), 0)
        wanted = jnp.zeros((block, n_dom), jnp.float32)
        for c in range(cap):
            wanted = jnp.where(row % cap == c, serve[c : c + 1, :], wanted)
        group = lax.broadcasted_iota(jnp.int32, (block, n_dom), 1)
        mine = group == row // (cap * n_local)
        index = jnp.sum(jnp.where(mine, wanted, 0.0), axis=1, keepdims=True).astype(jnp.int32)
        node = lax.broadcasted_iota(jnp.int32, (block, n_nodes), 1)
        chosen = jnp.where(node == index, 1.0, 0.0).astype(jnp.bfloat16)
        out_ref[base : base + block, :] = jnp.dot(
            chosen, features_ref[...], preferred_element_type=jnp.float32
        ).astype(jnp.bfloat16)


def local_kernel(
    n_local, cap, pick_ref, neighbours_ref, nodes_ref, features_ref, self_ref, counts_ref
):
    n_rows = counts_ref.shape[1]
    n_nodes = features_ref.shape[0]
    fanout, batch = neighbours_ref.shape
    pick = pick_ref[...]
    source = lax.broadcasted_iota(jnp.int32, pick.shape, 0)
    place = (pick // cap) * (n_local * cap) + source * cap + pick % cap
    nodes = nodes_ref[...].T
    for j in range(batch // LANES):
        rows = slice(j * LANES, (j + 1) * LANES)
        near = neighbours_ref[:, rows]
        lane, tile = near % LANES, near // LANES
        where = jnp.zeros_like(near)
        for m in range(pick.shape[0]):
            table = jnp.broadcast_to(place[m : m + 1, :], near.shape)
            found = jnp.take_along_axis(table, lane, axis=1)
            where = jnp.where(tile == m, found, where)
        for base in range(0, n_rows, LANES):
            row = base + lax.broadcasted_iota(jnp.int32, (LANES, LANES), 0)
            count = jnp.zeros((LANES, LANES), jnp.float32)
            for k in range(fanout):
                count += jnp.where(where[k : k + 1, :] == row, 1.0, 0.0)
            counts_ref[rows, base : base + LANES] = count.T.astype(jnp.bfloat16)
        node = lax.broadcasted_iota(jnp.int32, (LANES, n_nodes), 1)
        chosen = jnp.where(node == nodes[:, j : j + 1], 1.0, 0.0).astype(jnp.bfloat16)
        self_ref[rows, :] = jnp.dot(
            chosen, features_ref[...], preferred_element_type=jnp.float32
        ).astype(jnp.bfloat16)


def layer_kernel(
    fanout,
    scale,
    arrived_ref,
    counts_ref,
    self_ref,
    w_self_ref,
    w_neigh_ref,
    cotangent_ref,
    hidden_ref,
    partial_ref,
    inputs_ref,
    slope_ref,
    weights_ref,
):
    width = self_ref.shape[1]
    batch, units = cotangent_ref.shape
    weights_ref[:width, :] = w_self_ref[...]
    weights_ref[width:, :] = w_neigh_ref[...]
    step = 256
    for base in range(0, batch, step):
        rows = slice(base, base + step)
        inputs_ref[rows, :width] = self_ref[rows, :]
        total = jnp.dot(counts_ref[rows, :], arrived_ref[...], preferred_element_type=jnp.float32)
        inputs_ref[rows, width:] = (total * (1.0 / fanout)).astype(jnp.bfloat16)
        pre = jnp.dot(inputs_ref[rows, :], weights_ref[...], preferred_element_type=jnp.float32)
        sigma = jax.nn.sigmoid(pre)
        hidden_ref[rows, :] = (pre * sigma).astype(jnp.bfloat16)
        slope_ref[rows, :] = (
            cotangent_ref[rows, :].astype(jnp.float32) * sigma * (1.0 + pre * (1.0 - sigma))
        ).astype(jnp.bfloat16)
    terms = lax.dot_general(
        inputs_ref[...],
        slope_ref[...],
        (((0,), (0,)), ((), ())),
        preferred_element_type=jnp.float32,
    )
    terms = (terms * scale).astype(jnp.bfloat16)
    for i in range(units // LANES):
        partial_ref[i * 2 * width : (i + 1) * 2 * width, :] = terms[:, i * LANES : (i + 1) * LANES]


def unpack_kernel(packed_ref, grad_self_ref, grad_neigh_ref):
    width, units = grad_self_ref.shape
    for i in range(units // LANES):
        columns = slice(i * LANES, (i + 1) * LANES)
        base = i * 2 * width
        grad_self_ref[:, columns] = packed_ref[base : base + width, :].astype(jnp.float32)
        grad_neigh_ref[:, columns] = packed_ref[base + width : base + 2 * width, :].astype(
            jnp.float32
        )


def local(features, serve_rows, pick_rows, neighbours, batch_nodes, w_self, w_neigh, cotangent):
    n_dom = lax.axis_size("dom")
    n_local = lax.axis_size("local")
    n_devices = n_dom * n_local
    n_nodes, width = features.shape
    batch, fanout = neighbours.shape
    units = w_self.shape[1]
    cap = serve_rows.shape[1]
    n_rows = n_devices * cap
    bf16, f32 = jnp.bfloat16, jnp.float32
    struct = jax.ShapeDtypeStruct

    outgoing = call(
        functools.partial(serve_kernel, n_local),
        struct((n_rows, width), bf16),
        (serve_rows.T, features),
        2 * n_rows * n_nodes * width,
        2 * n_nodes * width,
    )
    arrived = lax.all_to_all(
        outgoing.reshape(n_devices, cap, width), AXES, split_axis=0, concat_axis=0, tiled=True
    ).reshape(n_rows, width)
    self_rows, counts = call(
        functools.partial(local_kernel, n_local, cap),
        (struct((batch, width), bf16), struct((batch, n_rows), bf16)),
        (pick_rows, neighbours.T, batch_nodes.reshape(-1, LANES), features),
        2 * batch * n_nodes * width,
        2 * n_nodes * width,
    )
    scale = 1.0 / math.sqrt(n_devices * batch)
    hidden, partial = call(
        functools.partial(layer_kernel, fanout, scale),
        (struct((batch, units), bf16), struct((2 * width * units // LANES, LANES), bf16)),
        (arrived, counts, self_rows, w_self, w_neigh, cotangent),
        8 * batch * width * units,
        4 * batch * units,
        (
            pltpu.VMEM((batch, 2 * width), bf16),
            pltpu.VMEM((batch, units), bf16),
            pltpu.VMEM((2 * width, units), bf16),
        ),
    )
    packed = partial.shape[0]
    share = -(-packed // n_devices)
    if share * n_devices != packed:
        partial = jnp.pad(partial, ((0, share * n_devices - packed), (0, 0)))
    pieces = lax.all_to_all(
        partial.reshape(n_devices, share, LANES), AXES, split_axis=0, concat_axis=0, tiled=True
    )
    summed = jnp.sum(pieces.astype(f32), axis=0).astype(bf16)
    gathered = lax.all_to_all(
        jnp.broadcast_to(summed, pieces.shape), AXES, split_axis=0, concat_axis=0, tiled=True
    ).reshape(n_devices * share, LANES)
    grad_self, grad_neigh = call(
        unpack_kernel,
        (struct((width, units), f32), struct((width, units), f32)),
        (gathered,),
        0,
        12 * width * units,
    )
    return hidden, grad_self, grad_neigh


def solution(mesh):
    rows = P(AXES, None)
    return jax.shard_map(
        local,
        mesh=mesh,
        in_specs=(rows, rows, rows, rows, P(AXES), P(), P(), rows),
        out_specs=(rows, P(), P()),
        check_vma=False,
    )
```

```python
import functools
import math

import jax
import jax.numpy as jnp
from jax import lax
from jax.experimental import pallas as pl
from jax.experimental.pallas import tpu as pltpu
from jax.sharding import PartitionSpec as P

AXES = ("dom", "local")
SENDS = ("local", "dom")
LANES = 128
CHUNKS = 4
STEP = 256
VMEM = pl.BlockSpec(memory_space=pltpu.VMEM)
HBM = pl.BlockSpec(memory_space=pltpu.HBM)


def call(
    kernel,
    out_shape,
    operands,
    flops,
    bytes_accessed,
    scratch=(),
    places=None,
    out=None,
    limit=40 * 2**20,
):
    return pl.pallas_call(
        kernel,
        out_shape=out_shape,
        in_specs=places or [VMEM] * len(operands),
        out_specs=out or jax.tree.map(lambda _: VMEM, out_shape),
        scratch_shapes=list(scratch),
        compiler_params=pltpu.CompilerParams(vmem_limit_bytes=limit),
        cost_estimate=pl.CostEstimate(
            flops=flops, bytes_accessed=bytes_accessed, transcendentals=0
        ),
    )(*operands)


def serve_kernel(serve_hbm, features_hbm, out_ref, serve_ref, features_ref, serve_sem, sems):
    cap, n_dom = serve_ref.shape
    n_nodes = features_ref.shape[0]
    part = n_nodes // CHUNKS
    fetch = pltpu.make_async_copy(serve_hbm, serve_ref, serve_sem)
    fetch.start()
    loads = []
    for i in range(CHUNKS):
        rows = pl.ds(i * part, part)
        loads.append(
            pltpu.make_async_copy(features_hbm.at[rows, :], features_ref.at[rows, :], sems.at[i])
        )
        loads[-1].start()
    fetch.wait()
    serve = serve_ref[...].astype(jnp.float32)
    block = LANES
    n_blocks = out_ref.shape[0] // block
    indices = []
    for b in range(n_blocks):
        row = b * block + lax.broadcasted_iota(jnp.int32, (block, n_dom), 0)
        wanted = jnp.zeros((block, n_dom), jnp.float32)
        for c in range(cap):
            wanted = jnp.where(row % cap == c, serve[c : c + 1, :], wanted)
        group = lax.broadcasted_iota(jnp.int32, (block, n_dom), 1)
        mine = group == row // cap % n_dom
        index = jnp.sum(jnp.where(mine, wanted, 0.0), axis=1, keepdims=True)
        indices.append(index.astype(jnp.int32))
    sums = [jnp.zeros((block, out_ref.shape[1]), jnp.float32)] * n_blocks
    for i in range(CHUNKS):
        loads[i].wait()
        node = i * part + lax.broadcasted_iota(jnp.int32, (block, part), 1)
        for b in range(n_blocks):
            chosen = jnp.where(node == indices[b], 1.0, 0.0).astype(jnp.bfloat16)
            sums[b] += jnp.dot(
                chosen, features_ref[i * part : (i + 1) * part, :], preferred_element_type=jnp.float32
            )
    for b in range(n_blocks):
        out_ref[b * block : (b + 1) * block, :] = sums[b].astype(jnp.bfloat16)


def local_kernel(pick_ref, neighbours_ref, nodes_ref, features_ref, self_ref, counts_ref):
    n_rows = counts_ref.shape[1]
    n_nodes = features_ref.shape[0]
    fanout, batch = neighbours_ref.shape
    pick = pick_ref[...]
    source = lax.broadcasted_iota(jnp.int32, pick.shape, 0)
    place = source * (n_rows // pick.shape[0]) + pick
    nodes = nodes_ref[...].T
    for j in range(batch // LANES):
        rows = slice(j * LANES, (j + 1) * LANES)
        near = neighbours_ref[:, rows]
        lane, tile = near % LANES, near // LANES
        where = jnp.zeros_like(near)
        for m in range(pick.shape[0]):
            table = jnp.broadcast_to(place[m : m + 1, :], near.shape)
            found = jnp.take_along_axis(table, lane, axis=1)
            where = jnp.where(tile == m, found, where)
        for base in range(0, n_rows, LANES):
            row = base + lax.broadcasted_iota(jnp.int32, (LANES, LANES), 0)
            count = jnp.zeros((LANES, LANES), jnp.float32)
            for k in range(fanout):
                count += jnp.where(where[k : k + 1, :] == row, 1.0, 0.0)
            counts_ref[rows, base : base + LANES] = count.T.astype(jnp.bfloat16)
        node = lax.broadcasted_iota(jnp.int32, (LANES, n_nodes), 1)
        chosen = jnp.where(node == nodes[:, j : j + 1], 1.0, 0.0).astype(jnp.bfloat16)
        self_ref[rows, :] = jnp.dot(
            chosen, features_ref[...], preferred_element_type=jnp.float32
        ).astype(jnp.bfloat16)


def layer_kernel(
    fanout,
    scale,
    arrived_ref,
    counts_ref,
    self_ref,
    w_self_ref,
    w_neigh_ref,
    cotangent_ref,
    hidden_hbm,
    partial_ref,
    inputs_ref,
    slope_ref,
    weights_ref,
    hidden_ref,
    sems,
):
    width = self_ref.shape[1]
    batch, units = cotangent_ref.shape
    weights_ref[:width, :] = w_self_ref[...]
    weights_ref[width:, :] = w_neigh_ref[...]
    copies = []
    for j in range(batch // STEP):
        rows = slice(j * STEP, (j + 1) * STEP)
        total = jnp.dot(counts_ref[rows, :], arrived_ref[...], preferred_element_type=jnp.float32)
        mean = (total * (1.0 / fanout)).astype(jnp.bfloat16)
        inputs = jnp.concatenate([self_ref[rows, :], mean], axis=1)
        inputs_ref[rows, :] = inputs
        pre = jnp.dot(inputs, weights_ref[...], preferred_element_type=jnp.float32)
        sigma = jax.nn.sigmoid(pre)
        hidden = pre * sigma
        hidden_ref[rows, :] = hidden.astype(jnp.bfloat16)
        copies.append(
            pltpu.make_async_copy(hidden_ref.at[rows, :], hidden_hbm.at[rows, :], sems.at[j])
        )
        copies[-1].start()
        slope_ref[rows, :] = (
            cotangent_ref[rows, :].astype(jnp.float32) * (sigma + hidden * (1.0 - sigma))
        ).astype(jnp.bfloat16)
    terms = lax.dot_general(
        inputs_ref[...],
        slope_ref[...],
        (((0,), (0,)), ((), ())),
        preferred_element_type=jnp.float32,
    )
    terms = (terms * scale).astype(jnp.bfloat16)
    for i in range(units // LANES):
        partial_ref[i * 2 * width : (i + 1) * 2 * width, :] = terms[:, i * LANES : (i + 1) * LANES]
    for copy in copies:
        copy.wait()


def unpack_kernel(packed_ref, grad_self_ref, grad_neigh_ref):
    width, units = grad_self_ref.shape
    for i in range(units // LANES):
        columns = slice(i * LANES, (i + 1) * LANES)
        base = i * 2 * width
        grad_self_ref[:, columns] = packed_ref[base : base + width, :].astype(jnp.float32)
        grad_neigh_ref[:, columns] = packed_ref[base + width : base + 2 * width, :].astype(
            jnp.float32
        )


def local(features, serve_rows, pick_rows, neighbours, batch_nodes, w_self, w_neigh, cotangent):
    n_dom = lax.axis_size("dom")
    n_local = lax.axis_size("local")
    n_devices = n_dom * n_local
    n_nodes, width = features.shape
    batch, fanout = neighbours.shape
    units = w_self.shape[1]
    cap = serve_rows.shape[1]
    n_rows = n_devices * cap
    bf16, f32 = jnp.bfloat16, jnp.float32
    struct = jax.ShapeDtypeStruct

    outgoing = call(
        serve_kernel,
        struct((n_rows, width), bf16),
        (serve_rows.T, features),
        2 * n_rows * n_nodes * width,
        2 * n_nodes * width,
        (
            pltpu.VMEM(serve_rows.shape[::-1], jnp.int32),
            pltpu.VMEM(features.shape, bf16),
            pltpu.SemaphoreType.DMA,
            pltpu.SemaphoreType.DMA((CHUNKS,)),
        ),
        [HBM, HBM],
        limit=60 * 2**20,
    )
    arrived = lax.all_to_all(
        outgoing.reshape(n_devices, cap, width), SENDS, split_axis=0, concat_axis=0, tiled=True
    ).reshape(n_rows, width)
    self_rows, counts = call(
        local_kernel,
        (struct((batch, width), bf16), struct((batch, n_rows), bf16)),
        (pick_rows, neighbours.T, batch_nodes.reshape(-1, LANES), features),
        2 * batch * n_nodes * width,
        2 * n_nodes * width,
    )
    scale = 1.0 / math.sqrt(n_devices * batch)
    hidden, partial = call(
        functools.partial(layer_kernel, fanout, scale),
        (struct((batch, units), bf16), struct((2 * width * units // LANES, LANES), bf16)),
        (arrived, counts, self_rows, w_self, w_neigh, cotangent),
        8 * batch * width * units,
        4 * batch * units,
        (
            pltpu.VMEM((batch, 2 * width), bf16),
            pltpu.VMEM((batch, units), bf16),
            pltpu.VMEM((2 * width, units), bf16),
            pltpu.VMEM((batch, units), bf16),
            pltpu.SemaphoreType.DMA((batch // STEP,)),
        ),
        out=(HBM, VMEM),
    )
    packed = partial.shape[0]
    share = -(-packed // n_devices)
    if share * n_devices != packed:
        partial = jnp.pad(partial, ((0, share * n_devices - packed), (0, 0)))
    pieces = lax.all_to_all(
        partial.reshape(n_devices, share, LANES), SENDS, split_axis=0, concat_axis=0, tiled=True
    )
    summed = jnp.sum(pieces.astype(f32), axis=0).astype(bf16)
    gathered = lax.all_to_all(
        jnp.broadcast_to(summed, pieces.shape), SENDS, split_axis=0, concat_axis=0, tiled=True
    ).reshape(n_devices * share, LANES)
    grad_self, grad_neigh = call(
        unpack_kernel,
        (struct((width, units), f32), struct((width, units), f32)),
        (gathered,),
        0,
        12 * width * units,
    )
    return hidden, grad_self, grad_neigh


def solution(mesh):
    rows = P(AXES, None)
    return jax.shard_map(
        local,
        mesh=mesh,
        in_specs=(rows, rows, rows, rows, P(AXES), P(), P(), rows),
        out_specs=(rows, P(), P()),
        check_vma=False,
    )
```

```python
import functools
import math

import jax
import jax.numpy as jnp
from jax import lax
from jax.experimental import pallas as pl
from jax.experimental.pallas import tpu as pltpu
from jax.sharding import PartitionSpec as P

AXES = ("dom", "local")
SENDS = ("local", "dom")
LANES = 128
STEP = 512
PARTS = 1
VMEM = pl.BlockSpec(memory_space=pltpu.VMEM)
HBM = pl.BlockSpec(memory_space=pltpu.HBM)


def call(
    kernel,
    out_shape,
    operands,
    flops,
    bytes_accessed,
    scratch=(),
    places=None,
    out=None,
):
    return pl.pallas_call(
        kernel,
        out_shape=out_shape,
        in_specs=places or [VMEM] * len(operands),
        out_specs=out or jax.tree.map(lambda _: VMEM, out_shape),
        scratch_shapes=list(scratch),
        compiler_params=pltpu.CompilerParams(vmem_limit_bytes=40 * 2**20),
        cost_estimate=pl.CostEstimate(
            flops=flops, bytes_accessed=bytes_accessed, transcendentals=0
        ),
    )(*operands)


def serve_kernel(
    serve_hbm,
    features_hbm,
    pick_hbm,
    neighbours_hbm,
    nodes_hbm,
    out_ref,
    features_ref,
    pick_ref,
    neighbours_ref,
    nodes_ref,
    serve_ref,
    sems,
):
    cap, n_dom = serve_ref.shape
    n_nodes = features_ref.shape[0]
    pairs = (
        (serve_hbm, serve_ref),
        (features_hbm, features_ref),
        (pick_hbm, pick_ref),
        (neighbours_hbm, neighbours_ref),
        (nodes_hbm, nodes_ref),
    )
    fetches = [pltpu.make_async_copy(*pair, sems.at[i]) for i, pair in enumerate(pairs)]
    for fetch in fetches:
        fetch.start()
    fetches[0].wait()
    serve = serve_ref[...].astype(jnp.float32)
    block = LANES
    picked = []
    for base in range(0, out_ref.shape[0], block):
        row = base + lax.broadcasted_iota(jnp.int32, (block, n_dom), 0)
        wanted = jnp.zeros((block, n_dom), jnp.float32)
        for c in range(cap):
            wanted = jnp.where(row % cap == c, serve[c : c + 1, :], wanted)
        group = lax.broadcasted_iota(jnp.int32, (block, n_dom), 1)
        mine = group == row // cap % n_dom
        index = jnp.sum(jnp.where(mine, wanted, 0.0), axis=1, keepdims=True).astype(jnp.int32)
        node = lax.broadcasted_iota(jnp.int32, (block, n_nodes), 1)
        picked.append(jnp.where(node == index, 1.0, 0.0).astype(jnp.bfloat16))
    for fetch in fetches[1:]:
        fetch.wait()
    for i, chosen in enumerate(picked):
        out_ref[i * block : (i + 1) * block, :] = jnp.dot(
            chosen, features_ref[...], preferred_element_type=jnp.float32
        ).astype(jnp.bfloat16)


def local_kernel(pick_ref, neighbours_ref, nodes_ref, features_ref, self_ref, counts_ref):
    n_rows = counts_ref.shape[1]
    n_nodes, width = features_ref.shape
    fanout, batch = neighbours_ref.shape
    bf16, i16 = jnp.bfloat16, jnp.int16
    one, zero = bf16(1), bf16(0)
    pick = pick_ref[...]
    source = lax.broadcasted_iota(jnp.int32, pick.shape, 0)
    place = source * (n_rows // pick.shape[0]) + pick
    nodes = nodes_ref[...].T
    half = n_nodes // 2
    halves = jnp.concatenate([features_ref[:half, :], features_ref[half:, :]], axis=1)
    node = lax.broadcasted_iota(jnp.int32, (LANES, half), 1)
    for j in range(batch // LANES):
        rows = slice(j * LANES, (j + 1) * LANES)
        near = neighbours_ref[:, rows]
        lane, tile = near % LANES, near // LANES
        where = jnp.zeros_like(near)
        for m in range(pick.shape[0]):
            table = jnp.broadcast_to(place[m : m + 1, :], near.shape)
            found = jnp.take_along_axis(table, lane, axis=1)
            where = jnp.where(tile == m, found, where)
        where = where.astype(i16)
        for base in range(0, n_rows, LANES):
            row = (base + lax.broadcasted_iota(jnp.int32, (LANES, LANES), 0)).astype(i16)
            count = jnp.zeros((LANES, LANES), bf16)
            for k in range(fanout):
                hit = jnp.broadcast_to(where[k : k + 1, :], (LANES, LANES)) == row
                count += jnp.where(hit, one, zero)
            counts_ref[rows, base : base + LANES] = count.T
        mine = nodes[:, j : j + 1]
        upper = mine >= half
        chosen = jnp.where(node == jnp.where(upper, mine - half, mine), 1.0, 0.0).astype(bf16)
        both = jnp.dot(chosen, halves, preferred_element_type=jnp.float32)
        self_ref[rows, :] = jnp.where(upper, both[:, width:], both[:, :width]).astype(bf16)


def layer_kernel(
    fanout,
    scale,
    arrived_ref,
    counts_ref,
    self_ref,
    w_self_ref,
    w_neigh_ref,
    cotangent_ref,
    hidden_ref,
    partial_ref,
    inputs_ref,
    slope_ref,
):
    width = self_ref.shape[1]
    batch, units = cotangent_ref.shape
    weights = jnp.concatenate([w_self_ref[...], w_neigh_ref[...]], axis=0)
    for base in range(0, batch, STEP):
        rows = slice(base, base + STEP)
        total = jnp.dot(counts_ref[rows, :], arrived_ref[...], preferred_element_type=jnp.float32)
        mean = (total * (1.0 / fanout)).astype(jnp.bfloat16)
        inputs = jnp.concatenate([self_ref[rows, :], mean], axis=1)
        inputs_ref[rows, :] = inputs
        pre = jnp.dot(inputs, weights, preferred_element_type=jnp.float32)
        sigma = jax.nn.sigmoid(pre)
        hidden = pre * sigma
        hidden_ref[rows, :] = hidden.astype(jnp.bfloat16)
        slope_ref[rows, :] = (
            cotangent_ref[rows, :].astype(jnp.float32) * (sigma + hidden * (1.0 - sigma))
        ).astype(jnp.bfloat16)
    terms = lax.dot_general(
        inputs_ref[...],
        slope_ref[...],
        (((0,), (0,)), ((), ())),
        preferred_element_type=jnp.float32,
    )
    terms = (terms * scale).astype(jnp.bfloat16)
    for i in range(units // LANES):
        partial_ref[i * 2 * width : (i + 1) * 2 * width, :] = terms[:, i * LANES : (i + 1) * LANES]


def finish_kernel(
    packed_ref, hidden_ref, hidden_hbm, grad_self_hbm, grad_neigh_hbm, grad_self_ref, grad_neigh_ref, sems
):
    width, units = grad_self_ref.shape
    part = hidden_ref.shape[0] // PARTS
    copies = []
    for i in range(PARTS):
        rows = pl.ds(i * part, part)
        copies.append(
            pltpu.make_async_copy(hidden_ref.at[rows, :], hidden_hbm.at[rows, :], sems.at[i])
        )
        copies[-1].start()
    for j, (ref, hbm) in enumerate(((grad_self_ref, grad_self_hbm), (grad_neigh_ref, grad_neigh_hbm))):
        for i in range(units // LANES):
            base = (2 * i + j) * width
            ref[:, i * LANES : (i + 1) * LANES] = packed_ref[base : base + width, :].astype(
                jnp.float32
            )
        copies.append(pltpu.make_async_copy(ref, hbm, sems.at[PARTS + j]))
        copies[-1].start()
    for copy in copies:
        copy.wait()


def local(features, serve_rows, pick_rows, neighbours, batch_nodes, w_self, w_neigh, cotangent):
    n_dom = lax.axis_size("dom")
    n_local = lax.axis_size("local")
    n_devices = n_dom * n_local
    n_nodes, width = features.shape
    batch, fanout = neighbours.shape
    units = w_self.shape[1]
    cap = serve_rows.shape[1]
    n_rows = n_devices * cap
    bf16, f32 = jnp.bfloat16, jnp.float32
    struct = jax.ShapeDtypeStruct

    own = (serve_rows.T, features, pick_rows, neighbours.T, batch_nodes.reshape(-1, LANES))
    held = [pltpu.VMEM(x.shape, x.dtype) for x in own]
    outgoing, *held = call(
        serve_kernel,
        (pltpu.VMEM((n_rows, width), bf16), held[1], held[2], held[3], held[4]),
        [pltpu.with_memory_space_constraint(x, pltpu.HBM) for x in own],
        2 * n_rows * n_nodes * width,
        2 * n_nodes * width,
        (held[0], pltpu.SemaphoreType.DMA((len(own),))),
        [HBM] * len(own),
    )
    arrived = lax.all_to_all(
        outgoing.reshape(n_devices, cap, width), SENDS, split_axis=0, concat_axis=0, tiled=True
    ).reshape(n_rows, width)
    self_rows, counts = call(
        local_kernel,
        (struct((batch, width), bf16), struct((batch, n_rows), bf16)),
        (held[1], held[2], held[3], held[0]),
        2 * batch * n_nodes * width,
        2 * n_nodes * width,
    )
    scale = 1.0 / math.sqrt(n_devices * batch)
    hidden, partial = call(
        functools.partial(layer_kernel, fanout, scale),
        (
            pltpu.VMEM((batch, units), bf16),
            pltpu.VMEM((2 * width * units // LANES, LANES), bf16),
        ),
        (arrived, counts, self_rows, w_self, w_neigh, cotangent),
        8 * batch * width * units,
        4 * batch * units,
        (pltpu.VMEM((batch, 2 * width), bf16), pltpu.VMEM((batch, units), bf16)),
    )
    packed = partial.shape[0]
    share = -(-packed // n_devices)
    if share * n_devices != packed:
        partial = jnp.pad(partial, ((0, share * n_devices - packed), (0, 0)))
    pieces = lax.all_to_all(
        partial.reshape(n_devices, share, LANES), SENDS, split_axis=0, concat_axis=0, tiled=True
    )
    summed = jnp.sum(pieces.astype(f32), axis=0).astype(bf16)
    gathered = lax.all_to_all(
        jnp.broadcast_to(summed, pieces.shape), SENDS, split_axis=0, concat_axis=0, tiled=True
    ).reshape(n_devices * share, LANES)
    grad = struct((width, units), f32)
    return call(
        finish_kernel,
        (struct(hidden.shape, bf16), grad, grad),
        (gathered, hidden),
        0,
        4 * batch * units + 12 * width * units,
        (
            pltpu.VMEM(grad.shape, f32),
            pltpu.VMEM(grad.shape, f32),
            pltpu.SemaphoreType.DMA((PARTS + 2,)),
        ),
        out=(HBM, HBM, HBM),
    )


def solution(mesh):
    rows = P(AXES, None)
    return jax.shard_map(
        local,
        mesh=mesh,
        in_specs=(rows, rows, rows, rows, P(AXES), P(), P(), rows),
        out_specs=(rows, P(), P()),
        check_vma=False,
    )
```

```python
import functools
import math

import jax
import jax.numpy as jnp
from jax import lax
from jax.experimental import pallas as pl
from jax.experimental.pallas import tpu as pltpu
from jax.sharding import PartitionSpec as P

AXES = ("dom", "local")
SENDS = ("local", "dom")
LANES = 128
VMEM = pl.BlockSpec(memory_space=pltpu.VMEM)
HBM = pl.BlockSpec(memory_space=pltpu.HBM)


def call(
    kernel,
    out_shape,
    operands,
    flops,
    bytes_accessed,
    scratch=(),
    places=None,
    out=None,
):
    return pl.pallas_call(
        kernel,
        out_shape=out_shape,
        in_specs=places or [VMEM] * len(operands),
        out_specs=out or jax.tree.map(lambda _: VMEM, out_shape),
        scratch_shapes=list(scratch),
        compiler_params=pltpu.CompilerParams(vmem_limit_bytes=40 * 2**20),
        cost_estimate=pl.CostEstimate(
            flops=flops, bytes_accessed=bytes_accessed, transcendentals=0
        ),
    )(*operands)


def serve_kernel(
    serve_hbm,
    features_hbm,
    pick_hbm,
    neighbours_hbm,
    nodes_hbm,
    out_ref,
    features_ref,
    pick_ref,
    neighbours_ref,
    nodes_ref,
    serve_ref,
    sems,
):
    cap, n_dom = serve_ref.shape
    n_nodes = features_ref.shape[0]
    pairs = (
        (serve_hbm, serve_ref),
        (features_hbm, features_ref),
        (pick_hbm, pick_ref),
        (neighbours_hbm, neighbours_ref),
        (nodes_hbm, nodes_ref),
    )
    fetches = [pltpu.make_async_copy(*pair, sems.at[i]) for i, pair in enumerate(pairs)]
    for fetch in fetches:
        fetch.start()
    fetches[0].wait()
    serve = serve_ref[...].astype(jnp.float32)
    block = LANES
    picked = []
    for base in range(0, out_ref.shape[0], block):
        row = base + lax.broadcasted_iota(jnp.int32, (block, n_dom), 0)
        wanted = jnp.zeros((block, n_dom), jnp.float32)
        for c in range(cap):
            wanted = jnp.where(row % cap == c, serve[c : c + 1, :], wanted)
        group = lax.broadcasted_iota(jnp.int32, (block, n_dom), 1)
        mine = group == row // cap % n_dom
        index = jnp.sum(jnp.where(mine, wanted, 0.0), axis=1, keepdims=True).astype(jnp.int32)
        node = lax.broadcasted_iota(jnp.int32, (block, n_nodes), 1)
        picked.append(jnp.where(node == index, 1.0, 0.0).astype(jnp.bfloat16))
    for fetch in fetches[1:]:
        fetch.wait()
    for i, chosen in enumerate(picked):
        out_ref[i * block : (i + 1) * block, :] = jnp.dot(
            chosen, features_ref[...], preferred_element_type=jnp.float32
        ).astype(jnp.bfloat16)


def local_kernel(pick_ref, neighbours_ref, nodes_ref, features_ref, self_ref, counts_ref):
    n_rows = counts_ref.shape[1]
    n_nodes, width = features_ref.shape
    fanout, batch = neighbours_ref.shape
    bf16, i16 = jnp.bfloat16, jnp.int16
    one, zero = bf16(1), bf16(0)
    pick = pick_ref[...]
    source = lax.broadcasted_iota(jnp.int32, pick.shape, 0)
    place = source * (n_rows // pick.shape[0]) + pick
    nodes = nodes_ref[...].T
    half = n_nodes // 2
    halves = jnp.concatenate([features_ref[:half, :], features_ref[half:, :]], axis=1)
    node = lax.broadcasted_iota(jnp.int32, (LANES, half), 1)
    for j in range(batch // LANES):
        rows = slice(j * LANES, (j + 1) * LANES)
        near = neighbours_ref[:, rows]
        lane, tile = near % LANES, near // LANES
        where = jnp.zeros_like(near)
        for m in range(pick.shape[0]):
            table = jnp.broadcast_to(place[m : m + 1, :], near.shape)
            found = jnp.take_along_axis(table, lane, axis=1)
            where = jnp.where(tile == m, found, where)
        where = where.astype(i16)
        for base in range(0, n_rows, LANES):
            row = (base + lax.broadcasted_iota(jnp.int32, (LANES, LANES), 0)).astype(i16)
            count = jnp.zeros((LANES, LANES), bf16)
            for k in range(fanout):
                hit = jnp.broadcast_to(where[k : k + 1, :], (LANES, LANES)) == row
                count += jnp.where(hit, one, zero)
            counts_ref[rows, base : base + LANES] = count.T
        mine = nodes[:, j : j + 1]
        upper = mine >= half
        chosen = jnp.where(node == jnp.where(upper, mine - half, mine), 1.0, 0.0).astype(bf16)
        both = jnp.dot(chosen, halves, preferred_element_type=jnp.float32)
        self_ref[rows, :] = jnp.where(upper, both[:, width:], both[:, :width]).astype(bf16)


def layer_kernel(
    fanout,
    scale,
    arrived_ref,
    counts_ref,
    self_ref,
    w_self_ref,
    w_neigh_ref,
    cotangent_ref,
    hidden_ref,
    partial_ref,
    inputs_ref,
    slope_ref,
):
    width = self_ref.shape[1]
    units = cotangent_ref.shape[1]
    weights = jnp.concatenate([w_self_ref[...], w_neigh_ref[...]], axis=0)
    total = jnp.dot(counts_ref[...], arrived_ref[...], preferred_element_type=jnp.float32)
    mean = (total * (1.0 / fanout)).astype(jnp.bfloat16)
    inputs = jnp.concatenate([self_ref[...], mean], axis=1)
    inputs_ref[...] = inputs
    pre = jnp.dot(inputs, weights, preferred_element_type=jnp.float32)
    sigma = jax.nn.sigmoid(pre)
    hidden = pre * sigma
    hidden_ref[...] = hidden.astype(jnp.bfloat16)
    slope_ref[...] = (
        cotangent_ref[...].astype(jnp.float32) * (sigma + hidden * (1.0 - sigma))
    ).astype(jnp.bfloat16)
    terms = lax.dot_general(
        inputs_ref[...],
        slope_ref[...],
        (((0,), (0,)), ((), ())),
        preferred_element_type=jnp.float32,
    )
    terms = (terms * scale).astype(jnp.bfloat16)
    for i in range(units // LANES):
        partial_ref[i * 2 * width : (i + 1) * 2 * width, :] = terms[:, i * LANES : (i + 1) * LANES]


def finish_kernel(
    packed_ref, hidden_ref, hidden_hbm, grad_self_hbm, grad_neigh_hbm, grad_self_ref, grad_neigh_ref, sems
):
    width, units = grad_self_ref.shape
    copies = [pltpu.make_async_copy(hidden_ref, hidden_hbm, sems.at[0])]
    copies[0].start()
    for j, (ref, hbm) in enumerate(((grad_self_ref, grad_self_hbm), (grad_neigh_ref, grad_neigh_hbm))):
        for i in range(units // LANES):
            base = (2 * i + j) * width
            ref[:, i * LANES : (i + 1) * LANES] = packed_ref[base : base + width, :].astype(
                jnp.float32
            )
        copies.append(pltpu.make_async_copy(ref, hbm, sems.at[1 + j]))
        copies[-1].start()
    for copy in copies:
        copy.wait()


def local(features, serve_rows, pick_rows, neighbours, batch_nodes, w_self, w_neigh, cotangent):
    n_dom = lax.axis_size("dom")
    n_local = lax.axis_size("local")
    n_devices = n_dom * n_local
    n_nodes, width = features.shape
    batch, fanout = neighbours.shape
    units = w_self.shape[1]
    cap = serve_rows.shape[1]
    n_rows = n_devices * cap
    bf16, f32 = jnp.bfloat16, jnp.float32
    struct = jax.ShapeDtypeStruct

    own = (serve_rows.T, features, pick_rows, neighbours.T, batch_nodes.reshape(-1, LANES))
    held = [pltpu.VMEM(x.shape, x.dtype) for x in own]
    outgoing, *held = call(
        serve_kernel,
        (pltpu.VMEM((n_rows, width), bf16), held[1], held[2], held[3], held[4]),
        [pltpu.with_memory_space_constraint(x, pltpu.HBM) for x in own],
        2 * n_rows * n_nodes * width,
        2 * n_nodes * width,
        (held[0], pltpu.SemaphoreType.DMA((len(own),))),
        [HBM] * len(own),
    )
    arrived = lax.all_to_all(
        outgoing.reshape(n_devices, cap, width), SENDS, split_axis=0, concat_axis=0, tiled=True
    ).reshape(n_rows, width)
    self_rows, counts = call(
        local_kernel,
        (struct((batch, width), bf16), struct((batch, n_rows), bf16)),
        (held[1], held[2], held[3], held[0]),
        2 * batch * n_nodes * width,
        2 * n_nodes * width,
    )
    scale = 1.0 / math.sqrt(n_devices * batch)
    hidden, partial = call(
        functools.partial(layer_kernel, fanout, scale),
        (
            pltpu.VMEM((batch, units), bf16),
            pltpu.VMEM((2 * width * units // LANES, LANES), bf16),
        ),
        (arrived, counts, self_rows, w_self, w_neigh, cotangent),
        8 * batch * width * units,
        4 * batch * units,
        (pltpu.VMEM((batch, 2 * width), bf16), pltpu.VMEM((batch, units), bf16)),
    )
    packed = partial.shape[0]
    share = -(-packed // n_devices)
    if share * n_devices != packed:
        partial = jnp.pad(partial, ((0, share * n_devices - packed), (0, 0)))
    pieces = lax.all_to_all(
        partial.reshape(n_devices, share, LANES), SENDS, split_axis=0, concat_axis=0, tiled=True
    )
    summed = jnp.sum(pieces.astype(f32), axis=0).astype(bf16)
    gathered = lax.all_to_all(
        jnp.broadcast_to(summed, pieces.shape), SENDS, split_axis=0, concat_axis=0, tiled=True
    ).reshape(n_devices * share, LANES)
    grad = struct((width, units), f32)
    return call(
        finish_kernel,
        (struct(hidden.shape, bf16), grad, grad),
        (gathered, hidden),
        0,
        4 * batch * units + 12 * width * units,
        (
            pltpu.VMEM(grad.shape, f32),
            pltpu.VMEM(grad.shape, f32),
            pltpu.SemaphoreType.DMA((3,)),
        ),
        out=(HBM, HBM, HBM),
    )


def solution(mesh):
    rows = P(AXES, None)
    return jax.shard_map(
        local,
        mesh=mesh,
        in_specs=(rows, rows, rows, rows, P(AXES), P(), P(), rows),
        out_specs=(rows, P(), P()),
        check_vma=False,
    )
```

```python
import functools
import math

import jax
import jax.numpy as jnp
from jax import lax
from jax.experimental import pallas as pl
from jax.experimental.pallas import tpu as pltpu
from jax.sharding import PartitionSpec as P

AXES = ("dom", "local")
SENDS = ("local", "dom")
LANES = 128
VMEM = pl.BlockSpec(memory_space=pltpu.VMEM)
HBM = pl.BlockSpec(memory_space=pltpu.HBM)


def call(
    kernel,
    out_shape,
    operands,
    flops,
    bytes_accessed,
    scratch=(),
    places=None,
    out=None,
    aliases={},
):
    return pl.pallas_call(
        kernel,
        out_shape=out_shape,
        in_specs=places or [VMEM] * len(operands),
        out_specs=out or jax.tree.map(lambda _: VMEM, out_shape),
        scratch_shapes=list(scratch),
        input_output_aliases=aliases,
        compiler_params=pltpu.CompilerParams(vmem_limit_bytes=40 * 2**20),
        cost_estimate=pl.CostEstimate(
            flops=flops, bytes_accessed=bytes_accessed, transcendentals=0
        ),
    )(*operands)


def waits_first():
    return lax.axis_index("dom") < lax.axis_size("dom") * 6 // 8


def local_work(pick_ref, neighbours_ref, nodes_ref, features_ref, self_ref, counts_ref):
    n_rows = counts_ref.shape[1]
    n_nodes, width = features_ref.shape
    fanout, batch = neighbours_ref.shape
    bf16, i16 = jnp.bfloat16, jnp.int16
    one, zero = bf16(1), bf16(0)
    pick = pick_ref[...]
    source = lax.broadcasted_iota(jnp.int32, pick.shape, 0)
    place = source * (n_rows // pick.shape[0]) + pick
    nodes = nodes_ref[...].T
    half = n_nodes // 2
    halves = jnp.concatenate([features_ref[:half, :], features_ref[half:, :]], axis=1)
    node = lax.broadcasted_iota(jnp.int32, (LANES, half), 1).astype(i16)
    for j in range(batch // LANES):
        mine = nodes[:, j : j + 1]
        upper = mine >= half
        low = jnp.broadcast_to(jnp.where(upper, mine - half, mine), (LANES, LANES)).astype(i16)
        hit = node == jnp.concatenate([low] * (half // LANES), axis=1)
        both = jnp.dot(jnp.where(hit, one, zero), halves, preferred_element_type=jnp.float32)
        self_ref[j * LANES : (j + 1) * LANES, :] = jnp.where(
            upper, both[:, width:], both[:, :width]
        ).astype(bf16)
    for j in range(batch // LANES):
        rows = slice(j * LANES, (j + 1) * LANES)
        near = neighbours_ref[:, rows]
        lane, tile = near & (LANES - 1), near // LANES
        where = jnp.zeros_like(near)
        for m in range(pick.shape[0]):
            table = jnp.broadcast_to(place[m : m + 1, :], near.shape)
            found = jnp.take_along_axis(table, lane, axis=1)
            where = jnp.where(tile == m, found, where)
        where = where.astype(i16)
        for base in range(0, n_rows, LANES):
            row = (base + lax.broadcasted_iota(jnp.int32, (LANES, LANES), 0)).astype(i16)
            hits = [
                jnp.where(jnp.broadcast_to(where[k : k + 1, :], row.shape) == row, one, zero)
                for k in range(fanout)
            ]
            while len(hits) > 1:
                odd = hits[len(hits) // 2 * 2 :]
                hits = [x + y for x, y in zip(hits[::2], hits[1::2])] + odd
            counts_ref[rows, base : base + LANES] = hits[0].T


def serve_kernel(
    serve_hbm,
    features_hbm,
    pick_hbm,
    neighbours_hbm,
    nodes_hbm,
    out_ref,
    self_ref,
    counts_ref,
    features_ref,
    pick_ref,
    neighbours_ref,
    nodes_ref,
    serve_ref,
    sems,
):
    cap, n_dom = serve_ref.shape
    n_nodes = features_ref.shape[0]
    pairs = (
        (serve_hbm, serve_ref),
        (features_hbm, features_ref),
        (pick_hbm, pick_ref),
        (neighbours_hbm, neighbours_ref),
        (nodes_hbm, nodes_ref),
    )
    fetches = [pltpu.make_async_copy(*pair, sems.at[i]) for i, pair in enumerate(pairs)]
    for fetch in fetches:
        fetch.start()
    fetches[0].wait()
    serve = serve_ref[...].astype(jnp.float32)
    block = LANES
    picked = []
    for base in range(0, out_ref.shape[0], block):
        row = base + lax.broadcasted_iota(jnp.int32, (block, n_dom), 0)
        wanted = jnp.zeros((block, n_dom), jnp.float32)
        for c in range(cap):
            wanted = jnp.where(row % cap == c, serve[c : c + 1, :], wanted)
        group = lax.broadcasted_iota(jnp.int32, (block, n_dom), 1)
        mine = group == row // cap % n_dom
        index = jnp.sum(jnp.where(mine, wanted, 0.0), axis=1, keepdims=True).astype(jnp.int32)
        node = lax.broadcasted_iota(jnp.int32, (block, n_nodes), 1)
        picked.append(jnp.where(node == index, 1.0, 0.0).astype(jnp.bfloat16))
    for fetch in fetches[1:]:
        fetch.wait()
    for i, chosen in enumerate(picked):
        out_ref[i * block : (i + 1) * block, :] = jnp.dot(
            chosen, features_ref[...], preferred_element_type=jnp.float32
        ).astype(jnp.bfloat16)

    @pl.when(waits_first())
    def _():
        local_work(pick_ref, neighbours_ref, nodes_ref, features_ref, self_ref, counts_ref)


def layer_kernel(
    fanout,
    scale,
    arrived_ref,
    early_self_ref,
    early_counts_ref,
    features_ref,
    pick_ref,
    neighbours_ref,
    nodes_ref,
    w_self_ref,
    w_neigh_ref,
    cotangent_ref,
    hidden_ref,
    partial_ref,
    self_ref,
    counts_ref,
    inputs_ref,
    slope_ref,
):
    width = self_ref.shape[1]
    units = cotangent_ref.shape[1]

    def layer():
        weights = jnp.concatenate([w_self_ref[...], w_neigh_ref[...]], axis=0)
        total = jnp.dot(counts_ref[...], arrived_ref[...], preferred_element_type=jnp.float32)
        mean = (total * (1.0 / fanout)).astype(jnp.bfloat16)
        inputs = jnp.concatenate([self_ref[...], mean], axis=1)
        inputs_ref[...] = inputs
        pre = jnp.dot(inputs, weights, preferred_element_type=jnp.float32)
        sigma = jax.nn.sigmoid(pre)
        hidden = pre * sigma
        hidden_ref[...] = hidden.astype(jnp.bfloat16)
        slope_ref[...] = (
            cotangent_ref[...].astype(jnp.float32) * (sigma + hidden * (1.0 - sigma))
        ).astype(jnp.bfloat16)
        terms = lax.dot_general(
            inputs_ref[...],
            slope_ref[...],
            (((0,), (0,)), ((), ())),
            preferred_element_type=jnp.float32,
        )
        terms = (terms * scale).astype(jnp.bfloat16)
        for i in range(units // LANES):
            partial_ref[i * 2 * width : (i + 1) * 2 * width, :] = terms[:, i * LANES : (i + 1) * LANES]

    first = waits_first()

    @pl.when(first)
    def _():
        layer()

    @pl.when(jnp.logical_not(first))
    def _():
        local_work(pick_ref, neighbours_ref, nodes_ref, features_ref, self_ref, counts_ref)
        layer()


def finish_kernel(
    packed_ref, hidden_ref, hidden_hbm, grad_self_hbm, grad_neigh_hbm, grad_self_ref, grad_neigh_ref, sems
):
    width, units = grad_self_ref.shape
    copies = [pltpu.make_async_copy(hidden_ref, hidden_hbm, sems.at[0])]
    copies[0].start()
    for j, (ref, hbm) in enumerate(((grad_self_ref, grad_self_hbm), (grad_neigh_ref, grad_neigh_hbm))):
        for i in range(units // LANES):
            base = (2 * i + j) * width
            ref[:, i * LANES : (i + 1) * LANES] = packed_ref[base : base + width, :].astype(
                jnp.float32
            )
        copies.append(pltpu.make_async_copy(ref, hbm, sems.at[1 + j]))
        copies[-1].start()
    for copy in copies:
        copy.wait()


def local(features, serve_rows, pick_rows, neighbours, batch_nodes, w_self, w_neigh, cotangent):
    n_dom = lax.axis_size("dom")
    n_local = lax.axis_size("local")
    n_devices = n_dom * n_local
    n_nodes, width = features.shape
    batch, fanout = neighbours.shape
    units = w_self.shape[1]
    cap = serve_rows.shape[1]
    n_rows = n_devices * cap
    bf16, f32 = jnp.bfloat16, jnp.float32
    struct = jax.ShapeDtypeStruct

    own = (serve_rows.T, features, pick_rows, neighbours.T, batch_nodes.reshape(-1, LANES))
    held = [pltpu.VMEM(x.shape, x.dtype) for x in own]
    outgoing, *held = call(
        serve_kernel,
        (
            pltpu.VMEM((n_rows, width), bf16),
            pltpu.VMEM((batch, width), bf16),
            pltpu.VMEM((batch, n_rows), bf16),
            *held[1:],
        ),
        [pltpu.with_memory_space_constraint(x, pltpu.HBM) for x in own],
        2 * (n_rows + batch) * n_nodes * width,
        2 * n_nodes * width,
        (held[0], pltpu.SemaphoreType.DMA((len(own),))),
        [HBM] * len(own),
    )
    outgoing, w_self, w_neigh, cotangent = lax.optimization_barrier(
        (outgoing, w_self, w_neigh, cotangent)
    )
    arrived = lax.all_to_all(
        outgoing.reshape(n_devices, cap, width), SENDS, split_axis=0, concat_axis=0, tiled=True
    ).reshape(n_rows, width)
    scale = 1.0 / math.sqrt(n_devices * batch)
    hidden, partial, _, _ = call(
        functools.partial(layer_kernel, fanout, scale),
        (
            pltpu.VMEM((batch, units), bf16),
            pltpu.VMEM((2 * width * units // LANES, LANES), bf16),
            pltpu.VMEM((batch, width), bf16),
            pltpu.VMEM((batch, n_rows), bf16),
        ),
        (arrived, *held, w_self, w_neigh, cotangent),
        8 * batch * width * units,
        4 * batch * units,
        (
            pltpu.VMEM((batch, 2 * width), bf16),
            pltpu.VMEM((batch, units), bf16),
        ),
        aliases={1: 2, 2: 3},
    )
    packed = partial.shape[0]
    share = -(-packed // n_devices)
    if share * n_devices != packed:
        partial = jnp.pad(partial, ((0, share * n_devices - packed), (0, 0)))
    pieces = lax.all_to_all(
        partial.reshape(n_devices, share, LANES), SENDS, split_axis=0, concat_axis=0, tiled=True
    )
    summed = jnp.sum(pieces.astype(f32), axis=0).astype(bf16)
    gathered = lax.all_to_all(
        jnp.broadcast_to(summed, pieces.shape), SENDS, split_axis=0, concat_axis=0, tiled=True
    ).reshape(n_devices * share, LANES)
    grad = struct((width, units), f32)
    return call(
        finish_kernel,
        (struct(hidden.shape, bf16), grad, grad),
        (gathered, hidden),
        0,
        4 * batch * units + 12 * width * units,
        (
            pltpu.VMEM(grad.shape, f32),
            pltpu.VMEM(grad.shape, f32),
            pltpu.SemaphoreType.DMA((3,)),
        ),
        out=(HBM, HBM, HBM),
    )


def solution(mesh):
    rows = P(AXES, None)
    return jax.shard_map(
        local,
        mesh=mesh,
        in_specs=(rows, rows, rows, rows, P(AXES), P(), P(), rows),
        out_specs=(rows, P(), P()),
        check_vma=False,
    )
```

```python
import functools
import math

import jax
import jax.numpy as jnp
from jax import lax
from jax.experimental import pallas as pl
from jax.experimental.pallas import tpu as pltpu
from jax.sharding import PartitionSpec as P

AXES = ("dom", "local")
SENDS = ("local", "dom")
LANES = 128
VMEM = pl.BlockSpec(memory_space=pltpu.VMEM)
HBM = pl.BlockSpec(memory_space=pltpu.HBM)


def call(
    kernel,
    out_shape,
    operands,
    flops,
    bytes_accessed,
    scratch=(),
    places=None,
    out=None,
):
    return pl.pallas_call(
        kernel,
        out_shape=out_shape,
        in_specs=places or [VMEM] * len(operands),
        out_specs=out or jax.tree.map(lambda _: VMEM, out_shape),
        scratch_shapes=list(scratch),
        compiler_params=pltpu.CompilerParams(vmem_limit_bytes=40 * 2**20),
        cost_estimate=pl.CostEstimate(
            flops=flops, bytes_accessed=bytes_accessed, transcendentals=0
        ),
    )(*operands)


def waits_first():
    return lax.axis_index("dom") < lax.axis_size("dom") // 2


def local_work(pick_ref, neighbours_ref, nodes_ref, features_ref, self_ref, counts_ref):
    n_rows = counts_ref.shape[1]
    n_nodes, width = features_ref.shape
    fanout, batch = neighbours_ref.shape
    bf16, i16 = jnp.bfloat16, jnp.int16
    one, zero = bf16(1), bf16(0)
    pick = pick_ref[...]
    source = lax.broadcasted_iota(jnp.int32, pick.shape, 0)
    place = source * (n_rows // pick.shape[0]) + pick
    nodes = nodes_ref[...].T
    half = n_nodes // 2
    halves = jnp.concatenate([features_ref[:half, :], features_ref[half:, :]], axis=1)
    node = lax.broadcasted_iota(jnp.int32, (LANES, half), 1).astype(i16)
    for j in range(batch // LANES):
        mine = nodes[:, j : j + 1]
        upper = mine >= half
        low = jnp.broadcast_to(jnp.where(upper, mine - half, mine), (LANES, LANES)).astype(i16)
        hit = node == jnp.concatenate([low] * (half // LANES), axis=1)
        both = jnp.dot(jnp.where(hit, one, zero), halves, preferred_element_type=jnp.float32)
        self_ref[j * LANES : (j + 1) * LANES, :] = jnp.where(
            upper, both[:, width:], both[:, :width]
        ).astype(bf16)
    for j in range(batch // LANES):
        rows = slice(j * LANES, (j + 1) * LANES)
        near = neighbours_ref[:, rows]
        lane, tile = near & (LANES - 1), near // LANES
        where = jnp.zeros_like(near)
        for m in range(pick.shape[0]):
            table = jnp.broadcast_to(place[m : m + 1, :], near.shape)
            found = jnp.take_along_axis(table, lane, axis=1)
            where = jnp.where(tile == m, found, where)
        where = where.astype(i16)
        for base in range(0, n_rows, LANES):
            row = (base + lax.broadcasted_iota(jnp.int32, (LANES, LANES), 0)).astype(i16)
            hits = [
                jnp.where(jnp.broadcast_to(where[k : k + 1, :], row.shape) == row, one, zero)
                for k in range(fanout)
            ]
            while len(hits) > 1:
                odd = hits[len(hits) // 2 * 2 :]
                hits = [x + y for x, y in zip(hits[::2], hits[1::2])] + odd
            counts_ref[rows, base : base + LANES] = hits[0].T


def serve_kernel(
    serve_hbm,
    features_hbm,
    pick_hbm,
    neighbours_hbm,
    nodes_hbm,
    out_ref,
    self_ref,
    counts_ref,
    features_ref,
    pick_ref,
    neighbours_ref,
    nodes_ref,
    serve_ref,
    sems,
):
    cap, n_dom = serve_ref.shape
    n_nodes = features_ref.shape[0]
    pairs = (
        (serve_hbm, serve_ref),
        (features_hbm, features_ref),
        (pick_hbm, pick_ref),
        (neighbours_hbm, neighbours_ref),
        (nodes_hbm, nodes_ref),
    )
    fetches = [pltpu.make_async_copy(*pair, sems.at[i]) for i, pair in enumerate(pairs)]
    for fetch in fetches:
        fetch.start()
    fetches[0].wait()
    serve = serve_ref[...].astype(jnp.float32)
    block = LANES
    picked = []
    for base in range(0, out_ref.shape[0], block):
        row = base + lax.broadcasted_iota(jnp.int32, (block, n_dom), 0)
        wanted = jnp.zeros((block, n_dom), jnp.float32)
        for c in range(cap):
            wanted = jnp.where(row % cap == c, serve[c : c + 1, :], wanted)
        group = lax.broadcasted_iota(jnp.int32, (block, n_dom), 1)
        mine = group == row // cap % n_dom
        index = jnp.sum(jnp.where(mine, wanted, 0.0), axis=1, keepdims=True).astype(jnp.int32)
        node = lax.broadcasted_iota(jnp.int32, (block, n_nodes), 1)
        picked.append(jnp.where(node == index, 1.0, 0.0).astype(jnp.bfloat16))
    for fetch in fetches[1:]:
        fetch.wait()
    for i, chosen in enumerate(picked):
        out_ref[i * block : (i + 1) * block, :] = jnp.dot(
            chosen, features_ref[...], preferred_element_type=jnp.float32
        ).astype(jnp.bfloat16)

    @pl.when(waits_first())
    def _():
        local_work(pick_ref, neighbours_ref, nodes_ref, features_ref, self_ref, counts_ref)


def layer_kernel(
    fanout,
    scale,
    arrived_ref,
    early_self_ref,
    early_counts_ref,
    features_ref,
    pick_ref,
    neighbours_ref,
    nodes_ref,
    w_self_ref,
    w_neigh_ref,
    cotangent_ref,
    hidden_ref,
    partial_ref,
    late_self_ref,
    late_counts_ref,
    inputs_ref,
    slope_ref,
):
    width = features_ref.shape[1]
    units = cotangent_ref.shape[1]

    def layer(self_ref, counts_ref):
        weights = jnp.concatenate([w_self_ref[...], w_neigh_ref[...]], axis=0)
        total = jnp.dot(counts_ref[...], arrived_ref[...], preferred_element_type=jnp.float32)
        mean = (total * (1.0 / fanout)).astype(jnp.bfloat16)
        inputs = jnp.concatenate([self_ref[...], mean], axis=1)
        inputs_ref[...] = inputs
        pre = jnp.dot(inputs, weights, preferred_element_type=jnp.float32)
        sigma = jax.nn.sigmoid(pre)
        hidden = pre * sigma
        hidden_ref[...] = hidden.astype(jnp.bfloat16)
        slope_ref[...] = (
            cotangent_ref[...].astype(jnp.float32) * (sigma + hidden * (1.0 - sigma))
        ).astype(jnp.bfloat16)
        terms = lax.dot_general(
            inputs_ref[...],
            slope_ref[...],
            (((0,), (0,)), ((), ())),
            preferred_element_type=jnp.float32,
        )
        terms = (terms * scale).astype(jnp.bfloat16)
        for i in range(units // LANES):
            partial_ref[i * 2 * width : (i + 1) * 2 * width, :] = terms[:, i * LANES : (i + 1) * LANES]

    first = waits_first()

    @pl.when(first)
    def _():
        layer(early_self_ref, early_counts_ref)

    @pl.when(jnp.logical_not(first))
    def _():
        local_work(
            pick_ref, neighbours_ref, nodes_ref, features_ref, late_self_ref, late_counts_ref
        )
        layer(late_self_ref, late_counts_ref)


def finish_kernel(
    packed_ref, hidden_ref, hidden_hbm, grad_self_hbm, grad_neigh_hbm, grad_self_ref, grad_neigh_ref, sems
):
    width, units = grad_self_ref.shape
    copies = [pltpu.make_async_copy(hidden_ref, hidden_hbm, sems.at[0])]
    copies[0].start()
    for j, (ref, hbm) in enumerate(((grad_self_ref, grad_self_hbm), (grad_neigh_ref, grad_neigh_hbm))):
        for i in range(units // LANES):
            base = (2 * i + j) * width
            ref[:, i * LANES : (i + 1) * LANES] = packed_ref[base : base + width, :].astype(
                jnp.float32
            )
        copies.append(pltpu.make_async_copy(ref, hbm, sems.at[1 + j]))
        copies[-1].start()
    for copy in copies:
        copy.wait()


def local(features, serve_rows, pick_rows, neighbours, batch_nodes, w_self, w_neigh, cotangent):
    n_dom = lax.axis_size("dom")
    n_local = lax.axis_size("local")
    n_devices = n_dom * n_local
    n_nodes, width = features.shape
    batch, fanout = neighbours.shape
    units = w_self.shape[1]
    cap = serve_rows.shape[1]
    n_rows = n_devices * cap
    bf16, f32 = jnp.bfloat16, jnp.float32
    struct = jax.ShapeDtypeStruct

    own = (serve_rows.T, features, pick_rows, neighbours.T, batch_nodes.reshape(-1, LANES))
    held = [pltpu.VMEM(x.shape, x.dtype) for x in own]
    outgoing, *held = call(
        serve_kernel,
        (
            pltpu.VMEM((n_rows, width), bf16),
            pltpu.VMEM((batch, width), bf16),
            pltpu.VMEM((batch, n_rows), bf16),
            *held[1:],
        ),
        [pltpu.with_memory_space_constraint(x, pltpu.HBM) for x in own],
        2 * (n_rows + batch) * n_nodes * width,
        2 * n_nodes * width,
        (held[0], pltpu.SemaphoreType.DMA((len(own),))),
        [HBM] * len(own),
    )
    outgoing, w_self, w_neigh, cotangent = lax.optimization_barrier(
        (outgoing, w_self, w_neigh, cotangent)
    )
    arrived = lax.all_to_all(
        outgoing.reshape(n_devices, cap, width), SENDS, split_axis=0, concat_axis=0, tiled=True
    ).reshape(n_rows, width)
    scale = 1.0 / math.sqrt(n_devices * batch)
    hidden, partial = call(
        functools.partial(layer_kernel, fanout, scale),
        (
            pltpu.VMEM((batch, units), bf16),
            pltpu.VMEM((2 * width * units // LANES, LANES), bf16),
        ),
        (arrived, *held, w_self, w_neigh, cotangent),
        8 * batch * width * units,
        4 * batch * units,
        (
            pltpu.VMEM((batch, width), bf16),
            pltpu.VMEM((batch, n_rows), bf16),
            pltpu.VMEM((batch, 2 * width), bf16),
            pltpu.VMEM((batch, units), bf16),
        ),
    )
    packed = partial.shape[0]
    share = -(-packed // n_devices)
    if share * n_devices != packed:
        partial = jnp.pad(partial, ((0, share * n_devices - packed), (0, 0)))
    pieces = lax.all_to_all(
        partial.reshape(n_devices, share, LANES), SENDS, split_axis=0, concat_axis=0, tiled=True
    )
    summed = jnp.sum(pieces.astype(f32), axis=0).astype(bf16)
    gathered = lax.all_to_all(
        jnp.broadcast_to(summed, pieces.shape), SENDS, split_axis=0, concat_axis=0, tiled=True
    ).reshape(n_devices * share, LANES)
    grad = struct((width, units), f32)
    return call(
        finish_kernel,
        (struct(hidden.shape, bf16), grad, grad),
        (gathered, hidden),
        0,
        4 * batch * units + 12 * width * units,
        (
            pltpu.VMEM(grad.shape, f32),
            pltpu.VMEM(grad.shape, f32),
            pltpu.SemaphoreType.DMA((3,)),
        ),
        out=(HBM, HBM, HBM),
    )


def solution(mesh):
    rows = P(AXES, None)
    return jax.shard_map(
        local,
        mesh=mesh,
        in_specs=(rows, rows, rows, rows, P(AXES), P(), P(), rows),
        out_specs=(rows, P(), P()),
        check_vma=False,
    )
```

```python
import functools
import math

import jax
import jax.numpy as jnp
from jax import lax
from jax.experimental import pallas as pl
from jax.experimental.pallas import tpu as pltpu
from jax.sharding import PartitionSpec as P

AXES = ("dom", "local")
SENDS = ("local", "dom")
LANES = 128
VMEM = pl.BlockSpec(memory_space=pltpu.VMEM)
HBM = pl.BlockSpec(memory_space=pltpu.HBM)


def call(
    kernel,
    out_shape,
    operands,
    flops,
    bytes_accessed,
    scratch=(),
    places=None,
    out=None,
):
    return pl.pallas_call(
        kernel,
        out_shape=out_shape,
        in_specs=places or [VMEM] * len(operands),
        out_specs=out or jax.tree.map(lambda _: VMEM, out_shape),
        scratch_shapes=list(scratch),
        compiler_params=pltpu.CompilerParams(vmem_limit_bytes=40 * 2**20),
        cost_estimate=pl.CostEstimate(
            flops=flops, bytes_accessed=bytes_accessed, transcendentals=0
        ),
    )(*operands)


def waits_first():
    return lax.axis_index("dom") < lax.axis_size("dom") // 2


def local_work(pick_ref, neighbours_ref, nodes_ref, features_ref, self_ref, counts_ref):
    n_rows = counts_ref.shape[1]
    n_nodes, width = features_ref.shape
    fanout, batch = neighbours_ref.shape
    bf16, i16 = jnp.bfloat16, jnp.int16
    one, zero = bf16(1), bf16(0)
    pick = pick_ref[...]
    source = lax.broadcasted_iota(jnp.int32, pick.shape, 0)
    place = source * (n_rows // pick.shape[0]) + pick
    nodes = nodes_ref[...].T
    half = n_nodes // 2
    halves = jnp.concatenate([features_ref[:half, :], features_ref[half:, :]], axis=1)
    node = lax.broadcasted_iota(jnp.int32, (LANES, half), 1).astype(i16)
    for j in range(batch // LANES):
        mine = nodes[:, j : j + 1]
        upper = mine >= half
        low = jnp.broadcast_to(jnp.where(upper, mine - half, mine), (LANES, LANES)).astype(i16)
        hit = node == jnp.concatenate([low] * (half // LANES), axis=1)
        both = jnp.dot(jnp.where(hit, one, zero), halves, preferred_element_type=jnp.float32)
        self_ref[j * LANES : (j + 1) * LANES, :] = jnp.where(
            upper, both[:, width:], both[:, :width]
        ).astype(bf16)
    for j in range(batch // LANES):
        rows = slice(j * LANES, (j + 1) * LANES)
        near = neighbours_ref[:, rows]
        lane, tile = near & (LANES - 1), near // LANES
        where = jnp.zeros_like(near)
        for m in range(pick.shape[0]):
            table = jnp.broadcast_to(place[m : m + 1, :], near.shape)
            found = jnp.take_along_axis(table, lane, axis=1)
            where = jnp.where(tile == m, found, where)
        where = where.astype(i16)
        for base in range(0, n_rows, LANES):
            row = (base + lax.broadcasted_iota(jnp.int32, (LANES, LANES), 0)).astype(i16)
            hits = [
                jnp.where(jnp.broadcast_to(where[k : k + 1, :], row.shape) == row, one, zero)
                for k in range(fanout)
            ]
            while len(hits) > 1:
                odd = hits[len(hits) // 2 * 2 :]
                hits = [x + y for x, y in zip(hits[::2], hits[1::2])] + odd
            counts_ref[rows, base : base + LANES] = hits[0].T


def serve_kernel(
    serve_hbm,
    features_hbm,
    pick_hbm,
    neighbours_hbm,
    nodes_hbm,
    out_ref,
    self_ref,
    counts_ref,
    features_ref,
    pick_ref,
    neighbours_ref,
    nodes_ref,
    serve_ref,
    sems,
):
    cap, n_dom = serve_ref.shape
    n_nodes, width = features_ref.shape
    half = n_nodes // 2
    pairs = (
        (features_hbm, features_ref),
        (serve_hbm, serve_ref),
        (pick_hbm, pick_ref),
        (neighbours_hbm, neighbours_ref),
        (nodes_hbm, nodes_ref),
    )
    fetches = [pltpu.make_async_copy(*pair, sems.at[i]) for i, pair in enumerate(pairs)]
    for fetch in fetches:
        fetch.start()
    fetches[1].wait()
    serve = serve_ref[...].astype(jnp.float32)
    block = LANES
    picked = []
    for base in range(0, out_ref.shape[0], block):
        row = base + lax.broadcasted_iota(jnp.int32, (block, n_dom), 0)
        wanted = jnp.zeros((block, n_dom), jnp.float32)
        for c in range(cap):
            wanted = jnp.where(row % cap == c, serve[c : c + 1, :], wanted)
        group = lax.broadcasted_iota(jnp.int32, (block, n_dom), 1)
        mine = group == row // cap % n_dom
        index = jnp.sum(jnp.where(mine, wanted, 0.0), axis=1, keepdims=True).astype(jnp.int32)
        upper = index >= half
        node = lax.broadcasted_iota(jnp.int32, (block, half), 1)
        hit = node == jnp.where(upper, index - half, index)
        picked.append((jnp.where(hit, 1.0, 0.0).astype(jnp.bfloat16), upper))
    fetches[0].wait()
    halves = jnp.concatenate([features_ref[:half, :], features_ref[half:, :]], axis=1)
    for i, (chosen, upper) in enumerate(picked):
        both = jnp.dot(chosen, halves, preferred_element_type=jnp.float32)
        out_ref[i * block : (i + 1) * block, :] = jnp.where(
            upper, both[:, width:], both[:, :width]
        ).astype(jnp.bfloat16)

    for fetch in fetches[2:]:
        fetch.wait()

    @pl.when(waits_first())
    def _():
        local_work(pick_ref, neighbours_ref, nodes_ref, features_ref, self_ref, counts_ref)


def layer_kernel(
    fanout,
    scale,
    arrived_ref,
    early_self_ref,
    early_counts_ref,
    features_ref,
    pick_ref,
    neighbours_ref,
    nodes_ref,
    w_self_ref,
    w_neigh_ref,
    cotangent_ref,
    hidden_ref,
    partial_ref,
    late_self_ref,
    late_counts_ref,
    inputs_ref,
    slope_ref,
):
    width = features_ref.shape[1]
    units = cotangent_ref.shape[1]

    def layer(self_ref, counts_ref):
        weights = jnp.concatenate([w_self_ref[...], w_neigh_ref[...]], axis=0)
        total = jnp.dot(counts_ref[...], arrived_ref[...], preferred_element_type=jnp.float32)
        mean = (total * (1.0 / fanout)).astype(jnp.bfloat16)
        inputs = jnp.concatenate([self_ref[...], mean], axis=1)
        inputs_ref[...] = inputs
        pre = jnp.dot(inputs, weights, preferred_element_type=jnp.float32)
        sigma = jax.nn.sigmoid(pre)
        hidden = pre * sigma
        hidden_ref[...] = hidden.astype(jnp.bfloat16)
        slope_ref[...] = (
            cotangent_ref[...].astype(jnp.float32) * (sigma + hidden * (1.0 - sigma))
        ).astype(jnp.bfloat16)
        terms = lax.dot_general(
            inputs_ref[...],
            slope_ref[...],
            (((0,), (0,)), ((), ())),
            preferred_element_type=jnp.float32,
        )
        terms = (terms * scale).astype(jnp.bfloat16)
        for i in range(units // LANES):
            partial_ref[i * 2 * width : (i + 1) * 2 * width, :] = terms[:, i * LANES : (i + 1) * LANES]

    first = waits_first()

    @pl.when(first)
    def _():
        layer(early_self_ref, early_counts_ref)

    @pl.when(jnp.logical_not(first))
    def _():
        local_work(
            pick_ref, neighbours_ref, nodes_ref, features_ref, late_self_ref, late_counts_ref
        )
        layer(late_self_ref, late_counts_ref)


def finish_kernel(
    packed_ref, hidden_ref, hidden_hbm, grad_self_hbm, grad_neigh_hbm, grad_self_ref, grad_neigh_ref, sems
):
    width, units = grad_self_ref.shape
    copies = [pltpu.make_async_copy(hidden_ref, hidden_hbm, sems.at[0])]
    copies[0].start()
    for j, (ref, hbm) in enumerate(((grad_self_ref, grad_self_hbm), (grad_neigh_ref, grad_neigh_hbm))):
        for i in range(units // LANES):
            base = (2 * i + j) * width
            ref[:, i * LANES : (i + 1) * LANES] = packed_ref[base : base + width, :].astype(
                jnp.float32
            )
        copies.append(pltpu.make_async_copy(ref, hbm, sems.at[1 + j]))
        copies[-1].start()
    for copy in copies:
        copy.wait()


def exchange_order(n_dom, n_local):
    def place(i):
        dom, local = divmod(i, n_local)
        return local // 2, dom % 2, (dom // 2) ^ 1, local % 2

    return sorted(range(n_dom * n_local), key=place)


def local(features, serve_rows, pick_rows, neighbours, batch_nodes, w_self, w_neigh, cotangent):
    n_dom = lax.axis_size("dom")
    n_local = lax.axis_size("local")
    n_devices = n_dom * n_local
    n_nodes, width = features.shape
    batch, fanout = neighbours.shape
    units = w_self.shape[1]
    cap = serve_rows.shape[1]
    n_rows = n_devices * cap
    bf16, f32 = jnp.bfloat16, jnp.float32
    struct = jax.ShapeDtypeStruct

    own = (serve_rows.T, features, pick_rows, neighbours.T, batch_nodes.reshape(-1, LANES))
    held = [pltpu.VMEM(x.shape, x.dtype) for x in own]
    outgoing, *held = call(
        serve_kernel,
        (
            pltpu.VMEM((n_rows, width), bf16),
            pltpu.VMEM((batch, width), bf16),
            pltpu.VMEM((batch, n_rows), bf16),
            *held[1:],
        ),
        [pltpu.with_memory_space_constraint(x, pltpu.HBM) for x in own],
        2 * (n_rows + batch) * n_nodes * width,
        2 * n_nodes * width,
        (held[0], pltpu.SemaphoreType.DMA((len(own),))),
        [HBM] * len(own),
    )
    outgoing, w_self, w_neigh, cotangent = lax.optimization_barrier(
        (outgoing, w_self, w_neigh, cotangent)
    )
    arrived = lax.all_to_all(
        outgoing.reshape(n_devices, cap, width), SENDS, split_axis=0, concat_axis=0, tiled=True
    ).reshape(n_rows, width)
    scale = 1.0 / math.sqrt(n_devices * batch)
    hidden, partial = call(
        functools.partial(layer_kernel, fanout, scale),
        (
            pltpu.VMEM((batch, units), bf16),
            pltpu.VMEM((2 * width * units // LANES, LANES), bf16),
        ),
        (arrived, *held, w_self, w_neigh, cotangent),
        8 * batch * width * units,
        4 * batch * units,
        (
            pltpu.VMEM((batch, width), bf16),
            pltpu.VMEM((batch, n_rows), bf16),
            pltpu.VMEM((batch, 2 * width), bf16),
            pltpu.VMEM((batch, units), bf16),
        ),
    )
    spread = {
        "split_axis": 0,
        "concat_axis": 0,
        "tiled": True,
        "axis_index_groups": [exchange_order(n_dom, n_local)],
    }
    packed = partial.shape[0]
    share = -(-packed // n_devices)
    if share * n_devices != packed:
        partial = jnp.pad(partial, ((0, share * n_devices - packed), (0, 0)))
    pieces = lax.all_to_all(
        partial.reshape(n_devices, share, LANES), AXES, **spread
    )
    summed = jnp.sum(pieces.astype(f32), axis=0).astype(bf16)
    gathered = lax.all_to_all(
        jnp.broadcast_to(summed, pieces.shape), AXES, **spread
    ).reshape(n_devices * share, LANES)
    grad = struct((width, units), f32)
    return call(
        finish_kernel,
        (struct(hidden.shape, bf16), grad, grad),
        (gathered, hidden),
        0,
        4 * batch * units + 12 * width * units,
        (
            pltpu.VMEM(grad.shape, f32),
            pltpu.VMEM(grad.shape, f32),
            pltpu.SemaphoreType.DMA((3,)),
        ),
        out=(HBM, HBM, HBM),
    )


def solution(mesh):
    rows = P(AXES, None)
    return jax.shard_map(
        local,
        mesh=mesh,
        in_specs=(rows, rows, rows, rows, P(AXES), P(), P(), rows),
        out_specs=(rows, P(), P()),
        check_vma=False,
    )
```
